32 devices in a mesh: rows: 8 (over z, x), span: 4 (over y, core).
Axes of the slice: x: 2, y: 2, z: 4, core: 2. Of those that a mesh axis runs over, the one named last changes fastest.
Arguments:
- tokens: bfloat16 [8, 2048, 512], P('rows', 'span'), may hold values from -6 to 6
- segment_ids: int32 [8, 2048], P('rows', 'span'), may hold values from 0 to 5, as said below
- vectors: bfloat16 [8, 512], P('span', 'rows'), may hold values from -2 to 2
- w_query: bfloat16 [512, 512], P('rows', 'span'), may hold values from -0.4375 to 0.4375
- w_key: bfloat16 [512, 512], P('rows', 'span'), may hold values from -0.4375 to 0.4375
- w_value: bfloat16 [512, 512], P('rows', 'span'), may hold values from -0.25 to 0.25
- w_out: bfloat16 [512, 512], P('rows', 'span'), may hold values from -1 to 1
- w_up: bfloat16 [512, 2048], P('rows', 'span'), may hold values from -0.25 to 0.25
- w_down: bfloat16 [2048, 512], P('rows', 'span'), may hold values from -0.125 to 0.125
- ffn_bias: bfloat16 [2560], P(('rows', 'span')), may hold values from -3 to 3
- cotangent: bfloat16 [8, 2048, 512], P('rows', 'span'), may hold values from -6 to 6
Outputs:
- block_out: bfloat16 [8, 2048, 512], P('rows', 'span')
- grad_tokens: float32 [8, 2048, 512], P('rows', 'span')
- grad_vectors: float32 [8, 512], P('span', 'rows')
- grad_query: float32 [512, 512], P('rows', 'span')
- grad_key: float32 [512, 512], P('rows', 'span')
- grad_value: float32 [512, 512], P('rows', 'span')
- grad_out: float32 [512, 512], P('rows', 'span')
- grad_up: float32 [512, 2048], P('rows', 'span')
- grad_down: float32 [2048, 512], P('rows', 'span')
- grad_ffn_bias: float32 [2560], P(('rows', 'span'))
The draws below stay inside these ranges and needn't reach their ends.
Inputs may be any that keep to these rules, and one draw needn't show every extreme that they name: `segment_ids`: within a sequence the ids never fall until padding 0 fills its end.
All inputs are finite; a program needn't handle non-finite values.
Results may differ from the reference program's by a relative error of at most 0.017.
The reference program's roundings to bfloat16 on the way count: a program that leaves them out, or rounds other values in their place, can miss the bound.
Values may be sent and summed in bfloat16 or wider, within the bound.
A program may use at most 128 MiB of HBM per device.

```python
import math
import jax
import jax.numpy as jnp
from jax import lax

D = 512
HEADS = 8
FF = 2048
SPAN_TOK = 512
LEN = 2048
SEQUENCES = 8


def draw_segment_ids(key, part):
    key = jax.random.fold_in(key, 11)
    subkeys = jax.random.split(key, 5)
    positions = jnp.arange(LEN, dtype=jnp.int32)[None, :]
    doc_start = jax.random.randint(subkeys[0], (SEQUENCES, 1), 0, SPAN_TOK // 2, dtype=jnp.int32)
    real_stop = LEN - jax.random.randint(subkeys[1], (SEQUENCES, 1), 0, SPAN_TOK // 4, dtype=jnp.int32)
    doc_close = real_stop - jax.random.randint(subkeys[2], (SEQUENCES, 1), 0, SPAN_TOK // 4, dtype=jnp.int32)
    early_cut = jax.random.randint(subkeys[3], (SEQUENCES, 1), 0, SPAN_TOK // 2, dtype=jnp.int32) % (doc_start + 1)
    late_cut = doc_close + jax.random.randint(subkeys[4], (SEQUENCES, 1), 0, SPAN_TOK // 4, dtype=jnp.int32)
    doc_ids = 1 + (positions >= early_cut).astype(jnp.int32) + (positions >= doc_start).astype(jnp.int32)
    doc_ids = doc_ids + (positions >= doc_close).astype(jnp.int32) + (positions >= late_cut).astype(jnp.int32)
    return jnp.where(positions < real_stop, doc_ids, 0).astype(jnp.int32)


def draw_vectors(key, part):
    key = jax.random.fold_in(key, 7)
    gain_key, second = jax.random.split(key)
    gain_rows = jax.random.uniform(gain_key, (8, D), jnp.float32, 0.6, 1.4)
    biases = 0.5 * jax.random.truncated_normal(second, -4.0, 4.0, (8, D), jnp.float32)
    row_index = jnp.arange(8)[:, None]
    return jnp.where((row_index == 0) | (row_index == 6), gain_rows, biases).astype(jnp.bfloat16)


def strengthened(values, stream_key, source, target, shards_of, factor):
    def block_of(position):
        return (jnp.arange(values.shape[position]) // (values.shape[position] // shards_of)).reshape((-1,) + (1,) * (values.ndim - 1 - position))

    one_side = jax.random.permutation(stream_key, shards_of)[block_of(target)]
    second = (block_of(target) + shards_of // 2) % shards_of
    return jnp.where((block_of(source) == one_side) | (block_of(source) == second), factor * values, values)


def shard_levels(rng, dims, shards, smallest, top_value):
    level = 1.0
    for axis_at, shards_of in shards:
        draws = jax.random.uniform(jax.random.fold_in(jax.random.fold_in(rng, 6), axis_at), (shards_of,), jnp.float32, smallest / len(shards), top_value / len(shards))
        level = level * jnp.repeat(jnp.exp(draws), dims[axis_at] // shards_of).reshape((-1,) + (1,) * (len(dims) - 1 - axis_at))
    return level


def normal_values(rng, extent, scale, limit, pieces=(), held_as=jnp.bfloat16):
    values = scale * jax.random.normal(rng, extent, jnp.float32)
    if pieces:
        values = values * shard_levels(rng, extent, pieces, -0.22, 0.18)
    return jnp.clip(values, -limit, limit).astype(held_as)


def bell_draw_with(rng, shape, scale, reach, cuts, heavy, held_as=jnp.bfloat16):
    array = scale * jax.random.normal(rng, shape, jnp.float32)
    if cuts:
        array = array * shard_levels(rng, shape, cuts, -0.22, 0.18)
    return jnp.clip(strengthened(array, jax.random.fold_in(rng, 3), *heavy), -reach, reach).astype(held_as)


def setup_inputs(seed: int = 0) -> dict:
    streams_of = jax.random.split(jax.random.key(seed), 12)
    tokens = normal_values(streams_of[0], (SEQUENCES, LEN, D), 1.0, 6.0, ((0, 8), (1, 4)))
    segment_ids = draw_segment_ids(jax.random.fold_in(streams_of[11], 71), 0)
    vectors = draw_vectors(jax.random.fold_in(streams_of[11], 71), 0)
    w_query = normal_values(streams_of[3], (D, D), (D // 3) ** -0.5, 0.4375, ((0, 8), (1, 4)))
    w_key = normal_values(streams_of[4], (D, D), (D // 3) ** -0.5, 0.4375, ((0, 8), (1, 4)))
    w_value = normal_values(streams_of[5], (D, D), D ** -0.5, 0.25, ((0, 8), (1, 4)))
    w_out = normal_values(streams_of[6], (D, D), (D // 16) ** -0.5, 1.0, ((0, 8), (1, 4)))
    w_up = normal_values(streams_of[7], (D, FF), D ** -0.5, 0.25, ((0, 8), (1, 4)))
    w_down = normal_values(streams_of[8], (FF, D), FF ** -0.5, 0.125, ((0, 8), (1, 4)))
    ffn_bias = normal_values(streams_of[9], (FF + D,), 0.5, 3.0, ((0, 32),))
    cotangent = bell_draw_with(streams_of[10], (SEQUENCES, LEN, D), 1.0, 6.0, ((0, 8), (1, 4)), (0, 2, 8, 2.0))
    return dict(tokens=tokens, segment_ids=segment_ids, vectors=vectors, w_query=w_query, w_key=w_key, w_value=w_value, w_out=w_out, w_up=w_up, w_down=w_down, ffn_bias=ffn_bias, cotangent=cotangent)


@jax.custom_vjp
def low(v):
    return lax.optimization_barrier(v.astype(jnp.bfloat16)).astype(jnp.float32)

@jax.custom_vjp
def low_back(v):
    return v

def low_keep(v):
    return (low(v), None)

def low_pass(kept, grad):
    return (grad,)

def back_keep(v):
    return (v, None)

def back_low(kept, grad):
    return (low(grad),)
low.defvjp(low_keep, low_pass)
low_back.defvjp(back_keep, back_low)
EPSILON = 1e-05
LOG_TWO = math.log(2.0)
FLOOR = -1e+30
PRECISE = lax.Precision.HIGHEST
QUERY_FORM = ('spbihe', 'spbihe', 'snhe')
KEY_FORM = ('spjhe', 'spbjhe', 'sjhe')
SCORE_FORM = ('spbihj', 'spbihj', 'snhj')
WEIGHT_FORM = ('spbirhj', 'spbirhj', 'snrhj')
OUTPUT_FORM = ('spbirhe', 'spbirhe', 'snrhe')

def layer_norm(values, weight_row, bias_row):
    average = lax.optimization_barrier(jnp.mean(values, axis=-1, keepdims=True))
    centered = values - average
    variance = lax.optimization_barrier(jnp.mean(centered * centered, axis=-1, keepdims=True))
    return centered * lax.rsqrt(variance + EPSILON) * weight_row + bias_row

def coarse_ids(seg_ids):
    paired = seg_ids.reshape(seg_ids.shape[0], seg_ids.shape[1] // 2, 2)
    return jnp.where(paired[:, :, 0] == paired[:, :, 1], paired[:, :, 0], 0)

def split_rows(tensor, pattern):
    if pattern == 2:
        return tensor
    return tensor.reshape((tensor.shape[0], tensor.shape[1] // 32, 2, 16) + tensor.shape[2:])

def arrange_keys(tensor, pattern):
    if pattern == 0:
        return tensor.reshape((tensor.shape[0], tensor.shape[1] // 32, 32) + tensor.shape[2:])
    if pattern == 1:
        return split_rows(tensor, 1)[:, :, ::-1]
    return tensor

def key_ids(seg_ids, pattern, row_count):
    leading = seg_ids.shape[0]
    if pattern == 0:
        grouped = seg_ids.reshape(leading, row_count // 32, 1, 1, 32)
        spread = jnp.broadcast_to(grouped, (leading, row_count // 32, 2, 16, 32))
        return spread.reshape(leading, row_count, 32)
    if pattern == 1:
        grouped = seg_ids.reshape(leading, row_count // 32, 2, 16)[:, :, ::-1]
        spread = jnp.broadcast_to(grouped[:, :, :, None, :], (leading, row_count // 32, 2, 16, 16))
        return spread.reshape(leading, row_count, 16)
    return jnp.broadcast_to(seg_ids[:, None, :], (leading, row_count, 16))

def fine_scores(coarse, key_seg, fine_ids, height, pattern):
    copies = 2 ** height
    spread = jnp.repeat(coarse, copies, axis=1)
    key_spread = jnp.repeat(key_seg, copies, axis=1)
    allowed = (key_spread == fine_ids[:, :, None]) & (key_spread != 0)
    if pattern == 0:
        positions = jnp.arange(fine_ids.shape[1]) % 32
        allowed = allowed | (positions[:, None] == jnp.arange(32)[None, :])[None]
    return jnp.where(allowed[:, :, None, :], spread + height * LOG_TWO, FLOOR)

def weight_rows(fine_rows, pattern, row_count):
    copies = fine_rows.shape[1] // row_count
    if pattern == 2:
        return fine_rows.reshape((fine_rows.shape[0], row_count, copies) + fine_rows.shape[2:])
    return fine_rows.reshape((fine_rows.shape[0], row_count // 32, 2, 16, copies) + fine_rows.shape[2:])

def contract(formula, first_op, second_op):
    return jnp.einsum(formula, first_op, second_op, precision=PRECISE)

def coarsen(tensor):
    paired = tensor.reshape((tensor.shape[0], tensor.shape[1] // 2, 2) + tensor.shape[2:])
    return low(0.5 * (paired[:, :, 0] + paired[:, :, 1]))

def attend(queries, key_rows, values, seg_ids):
    height_count = (queries.shape[1] // 32).bit_length()
    scaling = queries.shape[-1] ** (-0.5)
    ladder = [(queries, key_rows, values, seg_ids)]
    for height in range(1, height_count):
        previous = ladder[-1]
        ladder.append((coarsen(previous[0]), coarsen(previous[1]), coarsen(previous[2]), coarse_ids(previous[3])))
    masked = []
    for height in range(height_count):
        level_q, level_k, level_v, level_ids = ladder[height]
        pattern = 0 if height == 0 else 1
        row_count = level_q.shape[1]
        raw_scores = contract(QUERY_FORM[pattern] + ',' + KEY_FORM[pattern] + '->' + SCORE_FORM[pattern], split_rows(level_q, pattern), arrange_keys(level_k, pattern))
        coarse = low_back(raw_scores.reshape(level_q.shape[:2] + raw_scores.shape[-2:]) * scaling)
        masked.append(fine_scores(coarse, key_ids(level_ids, pattern, row_count), seg_ids, height, pattern))
    log_total = jax.nn.logsumexp(jnp.concatenate(masked, axis=-1), axis=-1, keepdims=True)
    result = jnp.zeros(queries.shape, jnp.float32)
    for height in range(height_count):
        level_q, level_k, level_v, level_ids = ladder[height]
        pattern = 0 if height == 0 else 1
        weights = low(jnp.exp(masked[height] - log_total))
        mixture = contract(WEIGHT_FORM[pattern] + ',' + KEY_FORM[pattern] + '->' + OUTPUT_FORM[pattern], weight_rows(weights, pattern, level_q.shape[1]), arrange_keys(level_v, pattern))
        result = result + mixture.reshape(queries.shape)
    return result

def forward(params, tokens_row, seg_row):
    vectors, w_query, w_key, w_value, w_out, w_up, w_down, ffn_bias = params
    hidden_units = w_up.shape[1]
    head_shape = (1, tokens_row.shape[0], HEADS, tokens_row.shape[1] // HEADS)
    normed = low(layer_norm(tokens_row, vectors[0], vectors[1]))
    queries = low_back(low(jnp.dot(normed, w_query, precision=PRECISE) + vectors[2]))
    key_rows = low_back(low(jnp.dot(normed, w_key, precision=PRECISE) + vectors[3]))
    values = low_back(low(jnp.dot(normed, w_value, precision=PRECISE) + vectors[4]))
    attended = attend(queries.reshape(head_shape), key_rows.reshape(head_shape), values.reshape(head_shape), seg_row[None])
    attended = low_back(low(attended.reshape(tokens_row.shape)))
    branch = low_back(jnp.dot(attended, w_out, precision=PRECISE) + vectors[5])
    middle = tokens_row + branch
    normed2 = low(layer_norm(middle, vectors[6], vectors[7]))
    upward = low_back(jnp.dot(normed2, w_up, precision=PRECISE) + ffn_bias[:hidden_units])
    active = low_back(low(jax.nn.gelu(upward, approximate=True)))
    feed_out = low_back(jnp.dot(active, w_down, precision=PRECISE) + ffn_bias[hidden_units:])
    return middle + feed_out

def reference(tokens, segment_ids, vectors, w_query, w_key, w_value, w_out, w_up, w_down, ffn_bias, cotangent):
    params = tuple((argument.astype(jnp.float32) for argument in (vectors, w_query, w_key, w_value, w_out, w_up, w_down, ffn_bias)))
    token_rows = tokens.astype(jnp.float32)
    grad_rows = cotangent.astype(jnp.float32)

    def one_row(totals, row_data):
        tokens_row, seg_row, cot_row = row_data
        result, pullback = jax.vjp(lambda p, t: forward(p, t, seg_row), params, tokens_row)
        grad_params, grad_input = pullback(cot_row)
        totals = jax.tree.map(jnp.add, totals, grad_params)
        return (totals, (result.astype(jnp.bfloat16), grad_input))
    starting = jax.tree.map(jnp.zeros_like, params)
    totals, (outputs, input_grads) = lax.scan(one_row, starting, (token_rows, segment_ids, grad_rows))
    return (outputs, input_grads, totals[0], totals[1], totals[2], totals[3], totals[4], totals[5], totals[6], totals[7])
```

```python
import functools
import math

import jax
import jax.numpy as jnp
from jax import lax
from jax.experimental import pallas as pl
from jax.experimental.pallas import tpu as pltpu
from jax.sharding import PartitionSpec as P

HEADS = 8
EPSILON = 1e-05
LOG_TWO = math.log(2.0)
FLOOR = -1e30
MESH = pl.DeviceIdType.MESH
F32 = jnp.float32
BF16 = jnp.bfloat16
TOK = 512
GRP = 128
KEYS = 288
SEEN = 128
GELU_C = math.sqrt(2.0 / math.pi)


def nn(a, b):
    return lax.dot_general(a, b, (((1,), (0,)), ((), ())), preferred_element_type=F32)


def nt(a, b):
    return lax.dot_general(a, b, (((1,), (1,)), ((), ())), preferred_element_type=F32)


def tn(a, b):
    return lax.dot_general(a, b, (((0,), (0,)), ((), ())), preferred_element_type=F32)


def iota(shape, dim):
    return lax.broadcasted_iota(jnp.int32, shape, dim)


def average_matrix(h):
    r, c = iota((GRP, GRP), 0), iota((GRP, GRP), 1)
    low = 2 ** (h - 1) - 1
    hit = ((r >> h) == (c >> h)) & ((r & low) == (c & low))
    return jnp.where(hit, 0.5, 0.0).astype(BF16)


def pair_matrix(n):
    r, c = iota((n // 2, n), 0), iota((n // 2, n), 1)
    return jnp.where((c >> 1) == r, 0.5, 0.0).astype(BF16)


def group_matrix(h):
    r, c = iota((2 * GRP, 2 * GRP), 0), iota((2 * GRP, 2 * GRP), 1)
    return jnp.where((r >> h) == (c >> h), 2.0**-h, 0.0).astype(BF16)


def token_block(rows, lanes):
    return (iota((rows, lanes), 1) & (GRP - 1)) >> 5


def compress(dense):
    lanes = dense.shape[1]
    tb = token_block(32, lanes)
    level0 = dense[0:32]
    for p in range(1, 4):
        level0 = jnp.where(tb == p, dense[32 * p : 32 * p + 32], level0)
    tb = token_block(16, lanes)
    level1 = dense[128:144]
    for k in range(1, 4):
        level1 = jnp.where(tb == (k ^ 1), dense[128 + 16 * k : 144 + 16 * k], level1)
    level2 = jnp.where((tb >> 1) == 0, dense[208:224], dense[192:208])
    return jnp.concatenate([level0, level1, level2, dense[224:288]], axis=0)


def expand(seen):
    lanes = seen.shape[1]
    tb = token_block(32, lanes)
    parts = [jnp.where(tb == p, seen[0:32], 0.0) for p in range(4)]
    tb = token_block(16, lanes)
    parts += [jnp.where(tb == (k ^ 1), seen[32:48], 0.0) for k in range(4)]
    parts += [jnp.where((tb >> 1) == (k ^ 1), seen[48:64], 0.0) for k in range(2)]
    parts.append(seen[64:128])
    return jnp.concatenate(parts, axis=0).astype(BF16)


def two_heads(rows):
    first = iota(rows.shape, 1) < 64
    zero = jnp.zeros_like(rows)
    return jnp.concatenate([jnp.where(first, rows, zero), jnp.where(first, zero, rows)], axis=0)


def flip(i):
    return i + 1 - 2 * lax.rem(i, 2)


def row_sum(x):
    return jnp.sum(x, axis=0, keepdims=True)


GROUPS = ("small", "qkv", "out", "up", "down")
SHARDS = ("small", "q", "k", "v", "out", "up", "down")
SUMS = ("up", "down", "out", "qkv")
LEVELS = ((0, 128), (128, 192), (192, 224), (224, 240), (240, 256), (256, 272), (272, 288))


class Place:
    def __init__(self):
        rows, span = lax.axis_index("rows"), lax.axis_index("span")
        self.rows, self.span = rows, span
        self.z, self.x = lax.div(rows, 2), lax.rem(rows, 2)
        self.y, self.c = lax.div(span, 2), lax.rem(span, 2)
        z, x, y, c = self.z, self.x, self.y, self.c
        self.nx, self.ny, self.nc = 1 - x, 1 - y, 1 - c
        self.ahead = lambda k: lax.rem(z + k, 4)
        self.first = self.dev(z, x + self.nc * (1 - 2 * x), y + c * (1 - 2 * y), c)
        self.second = self.dev(z, x + c * (1 - 2 * x), y + self.nc * (1 - 2 * y), c)
        self.f = x + c * (y - x)
        self.g = y + c * (x - y)
        self.core = self.dev(z, x, y, self.nc)
        self.across_x = self.dev(z, self.nx, y, c)
        self.across_y = self.dev(z, x, self.ny, c)

    @staticmethod
    def dev(z, x, y, c):
        return {"rows": 2 * z + x, "span": 2 * y + c}


def lanes(i, width=128):
    if isinstance(i, int):
        return pl.ds(width * i, width)
    return pl.ds(pl.multiple_of(width * i, width), width)


def remote(src, dst, ss, rs, dev):
    return pltpu.make_async_remote_copy(
        src_ref=src, dst_ref=dst, send_sem=ss, recv_sem=rs, device_id=dev, device_id_type=MESH)


class Gather:
    def __init__(self, place, shards, small, w4, wup, wdn, sems):
        self.p, self.shards = place, dict(zip(SHARDS, shards))
        self.small, self.w4, self.wup, self.wdn = small, w4, wup, wdn
        self.zs, self.zr, self.bs, self.br, self.ds, self.dr, self.cs, self.cr, self.loc = sems
        self.sent, self.local = [], {}

    def piece(self, name, z, x, s):
        if name == "small":
            return self.small.at[z, x, s]
        if name == "up":
            return self.wup.at[s, z, x]
        if name == "down":
            return self.wdn.at[z, x, :, lanes(s)]
        return self.w4.at[("q", "k", "v", "out").index(name), z, x, :, lanes(s)]

    def column(self, name, x, s):
        if name == "small":
            return self.small.at[:, x, s]
        if name == "up":
            return self.wup.at[s, :, x]
        if name == "down":
            return self.wdn.at[:, x, :, lanes(s)]
        return self.w4.at[pl.ds(0, 3) if name == "qkv" else pl.ds(3, 1), :, x, :, lanes(s)]

    def parts(self, name):
        return ("q", "k", "v") if name == "qkv" else (name,)

    def go(self, copy):
        copy.start()
        self.sent.append(copy)

    def keep(self, name):
        p = self.p
        for part in self.parts(name):
            copy = pltpu.make_async_copy(
                self.shards[part], self.piece(part, p.z, p.x, p.span), self.loc.at[SHARDS.index(part)])
            copy.start()
            self.local[part] = copy

    def start(self, name):
        p = self.p
        for part in self.parts(name):
            i = SHARDS.index(part)
            for k in (1, 3, 2):
                self.go(remote(self.shards[part], self.piece(part, p.z, p.x, p.span), self.zs.at[i, k],
                               self.zr.at[i, p.z], p.dev(p.ahead(k), p.x, p.y, p.c)))

    def to_core(self, name, x, y):
        p, i = self.p, GROUPS.index(name)
        col = self.column(name, x, 2 * y + p.c)
        self.go(remote(col, col, self.cs.at[i, 2 * x + y], self.cr.at[i, 2 * x + y], p.core))

    def along_z(self, name):
        p, i = self.p, GROUPS.index(name)
        for part in self.parts(name):
            j = SHARDS.index(part)
            for k in (1, 3, 2):
                z = p.ahead(k)
                got = self.piece(part, z, p.x, p.span)
                remote(got, got, self.zs.at[j, k], self.zr.at[j, z], p.dev(z, p.x, p.y, p.c)).wait_recv()
            self.local[part].wait()
        col = self.column(name, p.x, p.span)
        self.go(remote(col, col, self.bs.at[i, 0], self.br.at[i, 0], p.across_x))
        self.go(remote(col, col, self.bs.at[i, 1], self.br.at[i, 1], p.across_y))
        self.to_core(name, p.x, p.y)

    def across(self, name):
        p, i = self.p, GROUPS.index(name)
        fx, fy = p.x + p.nc * (1 - 2 * p.x), p.y + p.c * (1 - 2 * p.y)
        col = self.column(name, fx, 2 * fy + p.c)
        remote(col, col, self.bs.at[i, p.c], self.br.at[i, p.c], p.first).wait_recv()
        self.go(remote(col, col, self.ds.at[i], self.dr.at[i], p.second))
        self.to_core(name, fx, fy)
        gx, gy = p.x + p.c * (1 - 2 * p.x), p.y + p.nc * (1 - 2 * p.y)
        col = self.column(name, gx, 2 * gy + p.c)
        remote(col, col, self.bs.at[i, p.nc], self.br.at[i, p.nc], p.second).wait_recv()
        self.to_core(name, gx, gy)

    def diagonal(self, name):
        p, i = self.p, GROUPS.index(name)
        col = self.column(name, p.nx, 2 * p.ny + p.c)
        remote(col, col, self.ds.at[i], self.dr.at[i], p.second).wait_recv()
        self.to_core(name, p.nx, p.ny)

    def whole(self, name):
        p, i = self.p, GROUPS.index(name)
        for x in range(2):
            for y in range(2):
                col = self.column(name, x, 2 * y + p.nc)
                remote(col, col, self.cs.at[i, 2 * x + y], self.cr.at[i, 2 * x + y], p.core).wait_recv()


class Scatter:
    def __init__(self, place, g4, gup, gdn, bufs, sems):
        self.p, self.g4, self.gup, self.gdn = place, g4, gup, gdn
        self.bufs = dict(zip(SUMS, (bufs[7 * i : 7 * i + 7] for i in range(4))))
        self.cs, self.cr, self.fs, self.fr, self.ss, self.sr, self.zs, self.zr = sems
        self.sent = []

    def half(self, name, s):
        if name == "up":
            return self.gup.at[pl.ds(s, 1)]
        if name == "down":
            return self.gdn.at[:, :, :, :, lanes(s)]
        return self.g4.at[pl.ds(0, 3) if name == "qkv" else pl.ds(3, 1), :, :, :, lanes(s)]

    def block(self, name, k, z, x, s):
        if name == "up":
            return self.gup[s, z, x]
        if name == "down":
            return self.gdn[0, z, x, :, lanes(s)]
        return self.g4[k if name == "qkv" else 3, z, x, :, lanes(s)]

    def go(self, copy):
        copy.start()
        self.sent.append(copy)

    def start(self, name):
        p, i = self.p, SUMS.index(name)
        for y in range(2):
            self.go(remote(self.half(name, 2 * y + p.nc), self.bufs[name][0].at[y], self.cs.at[i, y],
                           self.cr.at[i, y], p.core))

    def first(self, name):
        p, i = self.p, SUMS.index(name)
        near, hold, got1 = self.bufs[name][0:3]
        for y in range(2):
            remote(self.half(name, 2 * y + p.nc), near.at[y], self.cs.at[i, y], self.cr.at[i, y], p.core).wait_recv()
        for a in range(2):
            for b in range(2):
                x, y = a + p.c * (b - a), b + p.c * (a - b)

                @pl.loop(0, 4)
                def _(z):
                    for k in range(near.shape[1]):
                        hold[a, b, k, z] = self.block(name, k, z, x, 2 * y + p.c) + near[y, k, z, x]

        self.go(remote(hold.at[1 - p.f], got1, self.fs.at[i], self.fr.at[i], p.first))

    def second(self, name):
        p, i = self.p, SUMS.index(name)
        _, hold, got1, held, got2 = self.bufs[name][0:5]
        remote(hold.at[1 - p.f], got1, self.fs.at[i], self.fr.at[i], p.first).wait_recv()

        @pl.loop(0, 4)
        def _(z):
            for b in range(2):
                for k in range(held.shape[1]):
                    held[b, k, z] = hold[p.f, b, k, z] + got1[b, k, z]

        self.go(remote(held.at[1 - p.g], got2, self.ss.at[i], self.sr.at[i], p.second))

    def third(self, name):
        p, i = self.p, SUMS.index(name)
        held, got2, last, got3 = self.bufs[name][3:7]
        remote(held.at[1 - p.g], got2, self.ss.at[i], self.sr.at[i], p.second).wait_recv()

        @pl.loop(0, 4)
        def _(z):
            for k in range(last.shape[1]):
                last[z, k] = held[p.g, k, z] + got2[k, z]

        for k in (1, 3, 2):
            z = p.ahead(k)
            self.go(remote(last.at[z], got3.at[p.z], self.zs.at[i, k], self.zr.at[i, p.z], p.dev(z, p.x, p.y, p.c)))

    def finish(self, name, outs):
        p, i = self.p, SUMS.index(name)
        last, got3 = self.bufs[name][5:7]
        for k in (1, 3, 2):
            z = p.ahead(k)
            remote(last.at[z], got3.at[z], self.zs.at[i, k], self.zr.at[i, z], p.dev(z, p.x, p.y, p.c)).wait_recv()
        for k, out in enumerate(outs):
            total = last[p.z, k].astype(F32)
            for j in (1, 2, 3):
                total = total + got3[p.ahead(j), k].astype(F32)
            out[...] = total


class Nothing:
    sent = ()

    def __getattr__(self, name):
        return lambda *a: None


def layer_kernel(fused, *refs):
    refs = list(refs)

    def take(n):
        got = refs[:n]
        del refs[:n]
        return got

    if fused:
        tok_h, cot_h = take(2)
        shards = take(7)
        out, gtok = take(2)
        o_q, o_k, o_v, o_out, o_up, o_down, o_vec, o_bias = take(8)
        tok, cot, small, vec, bias, w4, wup, wdn, g4, gup, gdn, gvec, gbias, ids = take(14)
        gsems = take(9)
        rbufs = take(28)
        rsems = take(8)
        sm_part, sm_got, sm_far, sm_ss, sm_rs, sm_zs, sm_zr, tok_sem = take(8)
    else:
        tok, cot, ids0, vec, bias, w4, wup, wdn = take(8)
        out, gtok, gvec, gbias, g4, gup, gdn = take(7)
        (ids,) = take(1)
    (n1, r1, n2, r2, normed, middle, qrep, kv0, kvg, maskb, gmat, probs, att, dkvg, datt, dqt, dkv, acc,
     kv_send, kv_recv, far_send, near_recv, half_recv,
     kv_ss, kv_rs, near_ss, near_rs, half_ss, half_rs) = refs

    span = lax.axis_index("span")
    half = lax.div(span, 2)
    sibling = flip(span)
    other = 2 * (1 - half)
    rows_of = lambda i: pl.ds(pl.multiple_of(i * GRP, GRP), GRP)

    if fused:
        p = Place()
        ag = Gather(p, shards, small, w4, wup, wdn, gsems)
        rs = Scatter(p, g4, gup, gdn, rbufs, rsems)
        copies_in = [pltpu.make_async_copy(a, b, tok_sem.at[i]) for i, (a, b) in enumerate(((tok_h, tok), (cot_h, cot)))]
        ag.keep("small")
        copies_in[0].start()
        ag.keep("qkv")
    else:
        ag = rs = Nothing()

    barrier = pltpu.get_barrier_semaphore()
    greet = [{"span": lax.rem(span + k, 4)} for k in range(1, 4)]
    if fused:
        greet += [p.dev(p.ahead(k), p.x, p.y, p.c) for k in range(1, 4)] + [p.across_x]
    for dev in greet:
        pl.semaphore_signal(barrier, inc=1, device_id=dev, device_id_type=MESH)
    pl.semaphore_wait(barrier, len(greet))

    ag.start("small")
    ag.start("qkv")
    if fused:
        for name in ("out", "up", "down"):
            ag.keep(name)
        copies_in[1].start()
        copies_in[0].wait()

    @pl.loop(0, 4)
    def _(i):
        x = tok[rows_of(i), :].astype(F32)
        mean = jnp.mean(x, axis=-1, keepdims=True)
        cen = x - mean
        r = lax.rsqrt(jnp.mean(cen * cen, axis=-1, keepdims=True) + EPSILON)
        n1[rows_of(i), :] = cen * r
        r1[rows_of(i), :] = r

    ag.along_z("small")
    ag.along_z("qkv")
    ag.start("out")
    ag.start("up")
    for h in range(1, 7):
        gmat[h - 1] = group_matrix(h)
    ag.across("small")
    ag.across("qkv")
    ag.along_z("out")
    ag.start("down")
    ag.diagonal("small")
    ag.diagonal("qkv")
    ag.along_z("up")
    ag.across("out")
    ag.whole("small")
    if fused:
        unpack_small(p, small, vec, bias, ids)
    else:
        ids[0] = ids0[...]
    make_mask(span, ids, maskb)
    ag.whole("qkv")
    ag.diagonal("out")
    ag.along_z("down")

    @pl.loop(0, 4)
    def _(i):
        normed[rows_of(i), :] = (n1[rows_of(i), :] * vec[0:1, :] + vec[1:2, :]).astype(BF16)

    square = lambda w: w.reshape(512, 512)
    qrep[0] = (nn(normed[...], square(w4[0])) + vec[2:3, :]).astype(BF16)
    kv0[:, 0:512] = (nn(normed[...], square(w4[1])) + vec[3:4, :]).astype(BF16)
    kv0[:, 512:1024] = (nn(normed[...], square(w4[2])) + vec[4:5, :]).astype(BF16)
    ag.across("up")
    ag.whole("out")

    level = kv0[...]
    ladder = [level]
    for h in range(1, 6):
        level = nn(pair_matrix(TOK >> (h - 1)), level).astype(BF16)
        ladder.append(level)
    kv_send[...] = ladder[5]
    sends = []
    for k in range(1, 4):
        copy = remote(kv_send, kv_recv.at[span], kv_ss.at[k], kv_rs.at[span], {"span": lax.rem(span + k, 4)})
        copy.start()
        sends.append(copy)
    ag.across("down")
    ag.diagonal("up")
    for g in range(4):
        kvg[g, 0:128, :] = kv0[128 * g : 128 * g + 128, :]
        kvg[g, 128:192, :] = ladder[1][64 * g : 64 * g + 64]
        kvg[g, 192:224, :] = ladder[2][32 * g : 32 * g + 32]
        kvg[g, 224:240, :] = ladder[3][16 * (g ^ 1) : 16 * (g ^ 1) + 16]
        kvg[g, 240:256, :] = ladder[4][16 * ((g // 2) ^ 1) : 16 * ((g // 2) ^ 1) + 16]
    for h in range(1, 7):
        avg = average_matrix(h)
        for g in range(4):
            qrep[h, 128 * g : 128 * g + 128, :] = nn(avg, qrep[h - 1, 128 * g : 128 * g + 128, :]).astype(BF16)

    for k in range(1, 4):
        src = lax.rem(span + k, 4)
        remote(kv_send, kv_recv.at[src], kv_ss.at[k], kv_rs.at[src], {"span": src}).wait_recv()
    far = jnp.concatenate([kv_recv[other], kv_recv[other + 1]], axis=0)
    level6 = nn(pair_matrix(32), far).astype(BF16)
    near = kv_recv[sibling]
    for g in range(4):
        kvg[g, 256:272, :] = near
        kvg[g, 272:288, :] = level6

    def attend(g, pair):
        k_all = kvg[g, :, lanes(pair)]
        v_all = kvg[g, :, lanes(4 + pair)]
        dense = []
        for h, (lo, hi) in enumerate(LEVELS):
            q2 = two_heads(qrep[h, rows_of(g), lanes(pair)])
            dense.append(nt(k_all[lo:hi], q2))
        score = compress(jnp.concatenate(dense, axis=0)) * 0.125
        m = maskb[g]
        score = score + jnp.concatenate([m, m], axis=1)
        top = jnp.max(score, axis=0, keepdims=True)
        total = jnp.sum(jnp.exp(score - top), axis=0, keepdims=True)
        prob = jnp.exp(score - (top + jnp.log(total)))
        probs[4 * g + pair] = prob
        o = tn(v_all, expand(prob)).astype(BF16)
        base = pl.multiple_of(pair * 128, 128)
        att[pl.ds(base, 64), rows_of(g)] = o[0:64, 0:128]
        att[pl.ds(base + 64, 64), rows_of(g)] = o[64:128, 128:256]

    for quarter in range(4):

        @pl.loop(0, 4)
        def _(pair):
            attend(quarter, pair)

        if quarter == 0:
            ag.diagonal("down")
        if quarter == 1:
            ag.whole("up")

    middle[...] = tn(att[...], square(w4[3])) + vec[5:6, :]

    @pl.loop(0, 4)
    def _(i):
        x = middle[rows_of(i), :] + tok[rows_of(i), :].astype(F32)
        middle[rows_of(i), :] = x
        mean = jnp.mean(x, axis=-1, keepdims=True)
        cen = x - mean
        r = lax.rsqrt(jnp.mean(cen * cen, axis=-1, keepdims=True) + EPSILON)
        n = cen * r
        n2[rows_of(i), :] = n
        r2[rows_of(i), :] = r
        datt[rows_of(i), :] = (n * vec[6:7, :] + vec[7:8, :]).astype(BF16)

    ag.whole("down")
    if fused:
        copies_in[1].wait()

    acc[...] = jnp.zeros_like(acc)
    gbias[...] = jnp.zeros_like(gbias)
    normed2 = datt

    @pl.loop(0, 4)
    def _(j):
        up = square(wup[j])
        u = nn(normed2[...], up) + bias[pl.ds(j, 1), :]
        t = jnp.tanh(GELU_C * (u + 0.044715 * (u * u * u)))
        active = (0.5 * u * (1.0 + t)).astype(BF16)
        slope = 0.5 * (1.0 + t) + (0.5 * GELU_C) * u * (1.0 - t * t) * (1.0 + (3 * 0.044715) * (u * u))
        down = wdn[j].reshape(512, 512)
        middle[...] += nn(active, down)
        d_active = nt(cot[...], down).astype(BF16).astype(F32)
        d_up = (d_active * slope).astype(BF16)
        gdn[0, j] = tn(active, cot[...]).astype(BF16).reshape(2, 256, 512)
        gup[j] = tn(normed2[...], d_up).astype(BF16).reshape(4, 2, 64, 512)
        gbias[pl.ds(j, 1), :] = row_sum(d_up.astype(F32))
        acc[...] += nt(d_up, up)

    rs.start("up")
    rs.start("down")
    gbias[4:5, :] = row_sum(cot[...].astype(F32))
    out[...] = (middle[...] + bias[4:5, :]).astype(BF16)

    gvec[...] = jnp.zeros_like(gvec)

    def norm_back(dz, n, r, gain):
        dn = dz * gain
        a = jnp.mean(dn, axis=-1, keepdims=True)
        b = jnp.mean(dn * n, axis=-1, keepdims=True)
        return r * (dn - a - n * b)

    @pl.loop(0, 4)
    def _(i):
        dz = acc[rows_of(i), :]
        n = n2[rows_of(i), :]
        gvec[6:7, :] += row_sum(dz * n)
        gvec[7:8, :] += row_sum(dz)
        dm = cot[rows_of(i), :].astype(F32) + norm_back(dz, n, r2[rows_of(i), :], vec[6:7, :])
        acc[rows_of(i), :] = dm
        db = dm.astype(BF16)
        gvec[5:6, :] += row_sum(db.astype(F32))
        datt[rows_of(i), :] = db

    rs.first("up")
    d_branch = datt[...]
    g4[3] = nn(att[...], d_branch).astype(BF16).reshape(4, 2, 64, 512)
    rs.start("out")
    rs.first("down")
    datt[...] = nt(d_branch, square(w4[3])).astype(BF16)

    def attend_back(g, pair):
        k_all = kvg[g, :, lanes(pair)]
        v_all = kvg[g, :, lanes(4 + pair)]
        do2 = two_heads(datt[rows_of(g), lanes(pair)])
        prob = probs[4 * g + pair]
        dp = compress(nt(v_all, do2))
        inner = jnp.sum(prob * dp, axis=0, keepdims=True)
        ds = prob * (dp - inner)
        dkvg[g, :, lanes(4 + pair)] = nn(expand(prob), do2)
        ds_wide = expand(ds)
        for h, (lo, hi) in enumerate(LEVELS):
            q2 = two_heads(qrep[h, rows_of(g), lanes(pair)])
            dkvg[g, lo:hi, lanes(pair)] = nn(ds_wide[lo:hi], q2) * 0.125
        summed = [ds[0:32]]
        for h in range(1, 7):
            summed.append(nn(ds[16 + 16 * h : 32 + 16 * h].astype(BF16), gmat[h - 1]))
        dq = tn(k_all, expand(jnp.concatenate(summed, axis=0))) * 0.125
        dq = dq.astype(BF16)
        base = pl.multiple_of(pair * 128, 128)
        dqt[pl.ds(base, 64), rows_of(g)] = dq[0:64, 0:128]
        dqt[pl.ds(base + 64, 64), rows_of(g)] = dq[64:128, 128:256]

    for quarter in range(4):

        @pl.loop(0, 4)
        def _(pair):
            attend_back(quarter, pair)

        if quarter == 0:
            rs.first("out")
            rs.second("up")
        if quarter == 1:
            rs.second("down")
            rs.second("out")
        if quarter == 2:
            rs.third("up")
            rs.third("out")
        if quarter == 3:
            rs.third("down")

    far_send[0] = dkvg[0, 256:272] + dkvg[1, 256:272] + dkvg[2, 256:272] + dkvg[3, 256:272]
    far_send[1] = dkvg[0, 272:288] + dkvg[1, 272:288] + dkvg[2, 272:288] + dkvg[3, 272:288]
    copies = [remote(far_send.at[0], near_recv, near_ss, near_rs, {"span": sibling})]
    mine = lax.rem(span, 2)
    for k in range(2):
        copies.append(remote(far_send.at[1, pl.ds(8 * k, 8)], half_recv.at[mine], half_ss.at[k],
                             half_rs.at[mine], {"span": other + k}))
    for copy in copies:
        copy.start()

    dq_t = dqt[...]
    normed_t = jnp.transpose(normed[...])
    g4[0] = nt(normed_t, dq_t).astype(BF16).reshape(4, 2, 64, 512)
    d_normed = middle
    d_normed[...] = nt(jnp.transpose(dq_t), square(w4[0]))
    gvec[2:3, :] = nt(jnp.ones((8, TOK), BF16), dq_t)[0:1]

    if fused:
        rs.finish("up", [o_up])
        rs.finish("out", [o_out])

    copies[0].wait_recv()
    for k in range(2):
        remote(far_send.at[1, pl.ds(8 * k, 8)], half_recv.at[k], half_ss.at[k], half_rs.at[k],
               {"span": other + k}).wait_recv()

    def spread(rows):
        return jnp.repeat(0.5 * rows, 2, axis=0)

    run = near_recv[...] + spread(half_recv[0] + half_recv[1])
    run = jnp.concatenate([dkvg[2, 240:256] + dkvg[3, 240:256], dkvg[0, 240:256] + dkvg[1, 240:256]], axis=0) + spread(run)
    run = jnp.concatenate([dkvg[g ^ 1, 224:240] for g in range(4)], axis=0) + spread(run)
    run = jnp.concatenate([dkvg[g, 192:224] for g in range(4)], axis=0) + spread(run)
    dkv[0:256] = jnp.concatenate([dkvg[g, 128:192] for g in range(4)], axis=0) + spread(run)
    for g in range(4):
        run = dkvg[g, 0:128] + spread(dkv[64 * g : 64 * g + 64])
        kv0[128 * g : 128 * g + 128, :] = run.astype(BF16)

    dk, dv = kv0[:, 0:512], kv0[:, 512:1024]
    gvec[3:4, :] = row_sum(dk.astype(F32))
    gvec[4:5, :] = row_sum(dv.astype(F32))
    g4[1] = nn(normed_t, dk).astype(BF16).reshape(4, 2, 64, 512)
    g4[2] = nn(normed_t, dv).astype(BF16).reshape(4, 2, 64, 512)
    rs.start("qkv")
    d_normed[...] += nt(dk, square(w4[1])) + nt(dv, square(w4[2]))

    @pl.loop(0, 4)
    def _(i):
        dz = d_normed[rows_of(i), :]
        n = n1[rows_of(i), :]
        gvec[0:1, :] += row_sum(dz * n)
        gvec[1:2, :] += row_sum(dz)
        gtok[rows_of(i), :] = acc[rows_of(i), :] + norm_back(dz, n, r1[rows_of(i), :], vec[0:1, :])

    if fused:
        sm_part[0, 0:8] = gvec[...]
        sm_part[0, 8:16] = gbias[...]
        steps = [remote(sm_part.at[i], sm_got.at[i], sm_ss.at[i], sm_rs.at[i], dev)
                 for i, dev in enumerate((p.core, p.first, p.second))]
        steps[0].start()
        rs.first("qkv")
        steps[0].wait_recv()
        sm_part[1] = sm_part[0] + sm_got[0]
        steps[1].start()
        rs.finish("down", [o_down])
        rs.second("qkv")
        steps[1].wait_recv()
        sm_part[2] = sm_part[1] + sm_got[1]
        steps[2].start()
        rs.third("qkv")
        steps[2].wait_recv()
        sm_part[3] = sm_part[2] + sm_got[2]
        for k in (1, 3, 2):
            z = p.ahead(k)
            copy = remote(sm_part.at[3], sm_far.at[p.z], sm_zs.at[k], sm_zr.at[p.z], p.dev(z, p.x, p.y, p.c))
            copy.start()
            steps.append(copy)
        rs.finish("qkv", [o_q, o_k, o_v])
        total = sm_part[3]
        for k in (1, 3, 2):
            z = p.ahead(k)
            remote(sm_part.at[3], sm_far.at[z], sm_zs.at[k], sm_zr.at[z], p.dev(z, p.x, p.y, p.c)).wait_recv()
            total = total + sm_far[z]
        sm_part[4] = total
        pack_small(p, sm_part, o_vec, o_bias)
        sends = sends + steps

    for copy in list(ag.sent) + list(rs.sent) + sends + copies:
        copy.wait_send()


def unpack_small(p, small, vec, bias, ids):
    for z in range(4):
        for s in range(4):
            pair = small[z, 0, s] + pltpu.roll(small[z, 1, s], 64, 1)
            vec[2 * s : 2 * s + 2, 128 * z : 128 * z + 128] = pair[0:2]
    lane = iota((8, 128), 1)
    chunk = [jnp.zeros((8, 128), F32) for _ in range(20)]
    for d in range(32):
        z, x, s = d // 8, (d // 4) % 2, d % 4
        k, off = divmod(80 * d, 128)
        t = small[z, x, s]
        t = pltpu.roll(t, off, 1) if off else t
        chunk[k] = chunk[k] + jnp.where(lane >= off, t, 0.0)
        if off > 48:
            chunk[k + 1] = chunk[k + 1] + jnp.where(lane < off, t, 0.0)
    for k in range(20):
        bias[k // 4 : k // 4 + 1, 128 * (k % 4) : 128 * (k % 4) + 128] = chunk[k][2:3]
    for s in range(4):
        ids[0, 4 * s : 4 * s + 4, :] = small[p.z, p.x, s][3:7]


def pack_small(p, part, o_vec, o_bias):
    wide = part[4, 0:8, lanes(p.z)]
    v = wide[0:2]
    for s in range(1, 4):
        v = jnp.where(jnp.broadcast_to(p.span == s, v.shape), wide[2 * s : 2 * s + 2], v)
    v = jnp.where(jnp.broadcast_to(p.x == 0, v.shape), v, pltpu.roll(v, 64, 1))
    o_vec[...] = v[:, 0:64]
    start = 80 * (4 * p.rows + p.span)
    k, off = lax.div(start, 128), lax.rem(start, 128)

    def row(k):
        wide = part[4, 8:16, lanes(lax.rem(k, 4))]
        return row_sum(jnp.where(iota((8, 128), 0) == lax.div(k, 4), wide, 0.0))

    lane = iota((1, 128), 1)
    a = pltpu.roll(jnp.broadcast_to(row(k), (8, 128)), lax.rem(128 - off, 128), 1)[0:1]
    b = pltpu.roll(jnp.broadcast_to(row(k + 1), (8, 128)), lax.rem(128 - off, 128), 1)[0:1]
    o_bias[...] = jnp.where(lane < 128 - off, a, b)[:, 0:80]


def make_mask(span, ids, maskb):
    lane = iota((16, GRP), 1)
    level = ids[0]
    for h in range(1, 7):
        d = 2 ** (h - 1)
        mate = jnp.where((lane & d) == 0, pltpu.roll(level, GRP - d, 1), pltpu.roll(level, d, 1))
        level = jnp.where(level == mate, level, 0.0)
        ids[h] = level
    half = lax.div(span, 2)
    sib, other = flip(span), 2 * (1 - half)

    def keys_of(h, first_row, count):
        per = GRP >> h
        r, c = iota((count, GRP), 0), iota((count, GRP), 1)
        value = jnp.broadcast_to(ids[h, pl.ds(first_row, 1), :], (count, GRP))
        for i in range(1, count // per):
            value = jnp.where(r // per == i, jnp.broadcast_to(ids[h, pl.ds(first_row + i, 1), :], (count, GRP)), value)
        return jnp.sum(jnp.where(c == (r % per) * 2**h, value, 0.0), axis=1, keepdims=True)

    far = [keys_of(5, 4 * sib, 16), keys_of(6, 4 * other, 16)]
    for g in range(4):
        row = 4 * span + g
        token = ids[0, pl.ds(row, 1), :]
        columns = [keys_of(0, row, 128), keys_of(1, row, 64), keys_of(2, row, 32),
                   keys_of(3, 4 * span + (g ^ 1), 16), keys_of(4, 4 * span + 2 * ((g // 2) ^ 1), 16)] + far
        parts = []
        for h, column in enumerate(columns):
            n = column.shape[0]
            allowed = (column == token) & (column != 0.0)
            if h == 0:
                allowed = allowed | (iota((n, GRP), 0) == iota((n, GRP), 1))
            parts.append(jnp.where(allowed, h * LOG_TWO, FLOOR))
        maskb[g] = compress(jnp.concatenate(parts, axis=0))


def layer(fused, operands):
    shape = jax.ShapeDtypeStruct
    V, D = pltpu.VMEM, pltpu.SemaphoreType.DMA
    vmem, anywhere = pl.BlockSpec(memory_space=pltpu.VMEM), pl.BlockSpec(memory_space=pl.ANY)
    w_shapes = [((4, 4, 2, 64, 512), BF16), ((4, 4, 2, 64, 512), BF16), ((4, 2, 256, 512), BF16)]
    g_shapes = w_shapes[:2] + [((1, 4, 2, 256, 512), BF16)]
    outs = [shape((TOK, 512), BF16), shape((TOK, 512), F32)]
    if fused:
        outs += [shape((64, 128), F32)] * 4 + [shape((64, 512), F32), shape((256, 128), F32), shape((2, 64), F32),
                                              shape((1, 80), F32)]
        scratch = [V((TOK, 512), BF16), V((TOK, 512), BF16), V((4, 2, 4, 8, 128), F32), V((8, 512), F32), V((8, 512), F32)]
        scratch += [V(*s) for s in w_shapes] + [V(*s) for s in g_shapes]
        scratch += [V((8, 512), F32), V((8, 512), F32), V((7, 16, 128), F32)]
        scratch += [D((7, 4)), D((7, 4)), D((5, 2)), D((5, 2)), D((5,)), D((5,)), D((5, 4)), D((5, 4)), D((7,))]
        for k, m, n in ((1, 64, 512), (1, 256, 128), (1, 64, 128), (3, 64, 128)):
            scratch += [V((2, k, 4, 2, m, n), BF16), V((2, 2, k, 4, m, n), BF16), V((2, k, 4, m, n), BF16),
                        V((2, k, 4, m, n), BF16), V((k, 4, m, n), BF16), V((4, k, m, n), BF16), V((4, k, m, n), BF16)]
        scratch += [D((4, 2)), D((4, 2)), D((4,)), D((4,)), D((4,)), D((4,)), D((4, 4)), D((4, 4))]
        scratch += [V((5, 16, 512), F32), V((3, 16, 512), F32), V((4, 16, 512), F32), D((3,)), D((3,)), D((4,)), D((4,)), D((2,))]
        in_specs = [anywhere] * 9
    else:
        outs += [shape((8, 512), F32)] * 2 + [shape(*s) for s in g_shapes]
        scratch = [V((7, 16, 128), F32)]
        in_specs = [vmem] * 8
    scratch += [
        V((TOK, 512), F32), V((TOK, 1), F32), V((TOK, 512), F32), V((TOK, 1), F32), V((TOK, 512), BF16),
        V((TOK, 512), F32), V((7, TOK, 512), BF16), V((TOK, 1024), BF16), V((4, KEYS, 1024), BF16),
        V((4, SEEN, GRP), F32), V((6, 2 * GRP, 2 * GRP), BF16), V((16, SEEN, 256), F32), V((512, TOK), BF16),
        V((4, KEYS, 1024), F32), V((TOK, 512), BF16), V((512, TOK), BF16), V((256, 1024), F32), V((TOK, 512), F32),
        V((16, 1024), BF16), V((4, 16, 1024), BF16), V((2, 16, 1024), F32), V((16, 1024), F32), V((2, 8, 1024), F32),
        D((4,)), D((4,)), D(()), D(()), D((2,)), D((2,)),
    ]
    return pl.pallas_call(
        functools.partial(layer_kernel, fused),
        out_shape=outs,
        in_specs=in_specs,
        out_specs=[vmem] * len(outs),
        scratch_shapes=scratch,
        compiler_params=pltpu.CompilerParams(collective_id=0, has_side_effects=True, vmem_limit_bytes=VMEM_BYTES),
        name="layer",
    )(*operands)


VMEM_BYTES = 62 * 2**20


def shards_fused(tokens, segment_ids, vectors, w_query, w_key, w_value, w_out, w_up, w_down, ffn_bias, cotangent):
    tile = jnp.concatenate([
        jnp.pad(vectors.astype(F32), ((0, 0), (0, 64))),
        jnp.pad(ffn_bias.astype(F32), (0, 48))[None],
        segment_ids.astype(F32).reshape(4, 128),
        jnp.zeros((1, 128), F32)], axis=0)
    out, gtok, gq, gk, gv, go, gup, gdn, gvec, gbias = layer(True, [
        tokens.reshape(TOK, 512), cotangent.reshape(TOK, 512), tile, w_query, w_key, w_value, w_out, w_up, w_down])
    return (out.reshape(tokens.shape), gtok.reshape(tokens.shape), gvec, gq, gk, gv, go, gup, gdn, gbias.reshape(80))


def shards_apart(tokens, segment_ids, vectors, w_query, w_key, w_value, w_out, w_up, w_down, ffn_bias, cotangent):
    ids = lax.all_gather(segment_ids, "span", axis=1, tiled=True).astype(F32).reshape(16, 128)
    gather = lambda w: lax.all_gather(lax.all_gather(w, "span", axis=1, tiled=True), "rows", axis=0, tiled=True)
    w4 = jnp.stack([gather(w) for w in (w_query, w_key, w_value, w_out)]).reshape(4, 4, 2, 64, 512)
    wdn = gather(w_down).reshape(4, 2, 256, 512)
    wup = lax.all_gather(lax.all_gather(w_up, "span", axis=0), "rows", axis=1, tiled=True).reshape(4, 4, 2, 64, 512)
    vec = lax.all_gather(lax.all_gather(vectors, "span", axis=0, tiled=True), "rows", axis=1, tiled=True).astype(F32)
    bias = lax.all_gather(ffn_bias, ("rows", "span"), axis=0, tiled=True).astype(F32)
    bias = jnp.pad(bias.reshape(5, 512), ((0, 3), (0, 0)))
    out, gtok, gvec, gbias, g4, gup, gdn = layer(False, [
        tokens.reshape(TOK, 512), cotangent.reshape(TOK, 512), ids, vec, bias, w4, wup, wdn])

    def scatter(g):
        part = lax.psum_scatter(g.astype(F32), "rows", scatter_dimension=0, tiled=True)
        return lax.psum_scatter(part.astype(BF16), "span", scatter_dimension=1, tiled=True).astype(F32)

    g4 = g4.reshape(4, 512, 512)
    gup = jnp.swapaxes(gup.reshape(4, 512, 512), 0, 1).reshape(512, 2048)
    gvec = lax.psum_scatter(gvec, "rows", scatter_dimension=1, tiled=True)
    gvec = lax.psum_scatter(gvec, "span", scatter_dimension=0, tiled=True)
    gbias = lax.psum_scatter(gbias[0:5].reshape(-1), ("rows", "span"), scatter_dimension=0, tiled=True)
    return (out.reshape(tokens.shape), gtok.reshape(tokens.shape), gvec, scatter(g4[0]), scatter(g4[1]), scatter(g4[2]),
            scatter(g4[3]), scatter(gup), scatter(gdn.reshape(2048, 512)), gbias)


def solution(mesh):
    grid = P("rows", "span")
    seq = P("rows", "span", None)
    in_specs = (seq, grid, P("span", "rows"), grid, grid, grid, grid, grid, grid, P(("rows", "span")), seq)
    out_specs = (seq, seq, P("span", "rows"), grid, grid, grid, grid, grid, grid, P(("rows", "span")))
    shards = shards_fused if mesh.shape["rows"] == 8 and mesh.shape["span"] == 4 else shards_apart
    return jax.shard_map(shards, mesh=mesh, in_specs=in_specs, out_specs=out_specs, check_vma=False)
```
